32 devices in a mesh: groups: 2 (over y), lat: 4 (over z), chan: 2 (over x), rep: 2 (over core).
Axes of the slice: x: 2, y: 2, z: 4, core: 2. Of those that a mesh axis runs over, the one named last changes fastest.
Arguments:
- hidden_encoding: bfloat16 [4, 256, 384, 1024], P(('groups', 'rep'), 'chan', 'lat'), parts along dimension 0, may hold values from -12 to 12
- eigenvalues: float32 [256, 256, 2, 128], P('chan', 'lat'), may hold values from -1 to 1, as said below
- desired_spectra: bfloat16 [4, 6, 256, 256, 2, 128], P(('groups', 'rep'), None, 'chan', 'lat'), parts along dimension 0, may hold values from -4 to 4
Outputs:
- predicted_state: bfloat16 [4, 256, 384, 1024], P(('groups', 'rep'), 'chan', 'lat'), parts along dimension 0
- clipped_grad: float32 [512, 256, 2, 128], P(('groups', 'chan'), 'lat'), parts along dimension 0
- spectral_misfit: float32 [2], P('groups'), parts along dimension 0
The draws below stay inside these ranges and needn't reach their ends.
There are 2 independent parts, one for each index of `groups`. The reference program is written for one: setup_inputs(seed, part) draws one part's arguments, and reference() takes and returns one part's arrays. A program takes and returns all parts, laid end to end along the dimension named above; an argument that names none is the same for every part. Nothing has to cross between parts.
Inputs may be any that keep to these rules, and one draw needn't show every extreme that they name: Each pair (eigenvalues[c, k, 0, l], eigenvalues[c, k, 1, l]) is a complex number of modulus below one.
All inputs are finite; a program needn't handle non-finite values.
Results may differ from the reference program's by a relative error of at most 0.0074.
Values may be sent and summed in bfloat16 or wider, within the bound.
A program may use at most 384 MiB of HBM per device.

```python
import math
import jax
import jax.numpy as jnp
from jax import lax

HIDDEN_FEATURES = 256
PARALLEL_COUNT = 384
MERIDIAN_COUNT = 1024
K = 256
L = 128
LEADS = 6
BATCH = 2


def draw_eigenvalues(key, part):
    key = jax.random.fold_in(key, 11)
    first, second = jax.random.split(key)
    wave = (jnp.arange(K, dtype=jnp.float32) / K)[None, :, None]
    spread = jnp.exp(jax.random.uniform(first, (HIDDEN_FEATURES, K, L), jnp.float32, math.log(0.5), math.log(2.0)))
    decay = (0.05 + 0.5 * wave) * spread
    radius = jnp.exp(-decay)
    phase = jax.random.uniform(second, (HIDDEN_FEATURES, K, L), jnp.float32, -math.pi, math.pi)
    return jnp.stack([radius * jnp.cos(phase), radius * jnp.sin(phase)], axis=2)


def level_of(stream_key, dims, pieces, smallest, largest):
    level = 1.0
    for axis_at, shards_of in pieces:
        draws = jax.random.uniform(jax.random.fold_in(jax.random.fold_in(stream_key, 6), axis_at), (shards_of,), jnp.float32, smallest / len(pieces), largest / len(pieces))
        level = level * jnp.repeat(jnp.exp(draws), dims[axis_at] // shards_of).reshape((-1,) + (1,) * (len(dims) - 1 - axis_at))
    return level


def scatter_about(key, dims, scale, most, pieces=(), held_as=jnp.bfloat16):
    values = jax.random.normal(key, dims, jnp.float32) * scale
    if len(pieces) > 0:
        values = level_of(key, dims, pieces, -0.22, 0.18) * values
    return jnp.clip(values, min=-most, max=most).astype(held_as)


def setup_inputs(seed: int = 0, part: int = 0) -> dict:
    arg_keys = jax.random.split(jax.random.key(seed), 4)
    own_keys = jax.random.split(jax.random.fold_in(arg_keys[3], part), 4)
    hidden_encoding = scatter_about(own_keys[0], (BATCH, HIDDEN_FEATURES, PARALLEL_COUNT, MERIDIAN_COUNT), 2.0, 12.0, ((0, 2), (1, 2), (2, 4)))
    eigenvalues = draw_eigenvalues(jax.random.fold_in(arg_keys[3], 71), part)
    desired_spectra = scatter_about(own_keys[2], (BATCH, LEADS, HIDDEN_FEATURES, K, 2, L), 0.6, 4.0, ((0, 2), (2, 2), (3, 4)))
    return {"hidden_encoding": hidden_encoding, "eigenvalues": eigenvalues, "desired_spectra": desired_spectra}


def forward_table(wavenumber_span, kept):
    column = jnp.arange(wavenumber_span, dtype=jnp.int32)[:, None]
    wave = jnp.arange(kept, dtype=jnp.int32)[None, :]
    phase = (wave * column % wavenumber_span).astype(jnp.float32) * (2.0 * math.pi / wavenumber_span)
    factor = 1.0 / math.sqrt(wavenumber_span)
    table = jnp.stack([jnp.cos(phase) * factor, -jnp.sin(phase) * factor], axis=2)
    return table.reshape(wavenumber_span, 2 * kept)

def inverse_table(wavenumber_span, kept):
    wave = jnp.arange(kept, dtype=jnp.int32)[:, None]
    column = jnp.arange(wavenumber_span, dtype=jnp.int32)[None, :]
    phase = (wave * column % wavenumber_span).astype(jnp.float32) * (2.0 * math.pi / wavenumber_span)
    weight = jnp.where(wave == 0, 1.0, 2.0).astype(jnp.float32) / math.sqrt(wavenumber_span)
    table = jnp.stack([weight * jnp.cos(phase), -weight * jnp.sin(phase)], axis=1)
    return table.reshape(2 * kept, wavenumber_span)

def latitude_table(height, modes):
    row = jnp.arange(height, dtype=jnp.int32)[:, None]
    mode = jnp.arange(modes, dtype=jnp.int32)[None, :]
    phase = ((2 * row + 1) * mode % (4 * height)).astype(jnp.float32) * (math.pi / (2 * height))
    weight = jnp.where(mode == 0, math.sqrt(1.0 / height), math.sqrt(2.0 / height)).astype(jnp.float32)
    return weight * jnp.cos(phase)

def reference(hidden_encoding, eigenvalues, desired_spectra):
    ceiling_bound = lax.Precision.HIGHEST
    forward = forward_table(MERIDIAN_COUNT, K).astype(jnp.bfloat16).astype(jnp.float32)
    reverse_pass = inverse_table(MERIDIAN_COUNT, K).astype(jnp.bfloat16).astype(jnp.float32)
    basis = latitude_table(PARALLEL_COUNT, L)
    basis_half = basis.astype(jnp.bfloat16).astype(jnp.float32)
    lam_real = eigenvalues[:, :, 0]
    lam_imag = eigenvalues[:, :, 1]

    def one_example(pair):
        field, goals = pair
        vectorized_field = field.reshape(HIDDEN_FEATURES * PARALLEL_COUNT, MERIDIAN_COUNT).astype(jnp.float32)
        spectra = jnp.dot(vectorized_field, forward, precision=ceiling_bound).astype(jnp.bfloat16)
        spectra = spectra.reshape(HIDDEN_FEATURES, PARALLEL_COUNT, 2 * K).astype(jnp.float32)
        coeffs = jnp.einsum('chq,hl->cql', spectra, basis_half, precision=ceiling_bound)
        state = coeffs.reshape(HIDDEN_FEATURES, K, 2, L)
        subset_misfit = jnp.zeros((), jnp.float32)
        derivative_inphase = jnp.zeros((HIDDEN_FEATURES, K, L), jnp.float32)
        derivative_quadrature = jnp.zeros((HIDDEN_FEATURES, K, L), jnp.float32)
        for lead in range(LEADS):
            prev_real = state[:, :, 0]
            prev_imag = state[:, :, 1]
            next_real = lam_real * prev_real - lam_imag * prev_imag
            next_imag = lam_real * prev_imag + lam_imag * prev_real
            goal = goals[lead].astype(jnp.float32)
            res_real = next_real - goal[:, :, 0]
            res_imag = next_imag - goal[:, :, 1]
            subset_misfit = subset_misfit + jnp.sum(res_real * res_real + res_imag * res_imag)
            weight = 2.0 * (lead + 1)
            derivative_inphase = derivative_inphase + weight * (prev_real * res_real + prev_imag * res_imag)
            derivative_quadrature = derivative_quadrature + weight * (prev_real * res_imag - prev_imag * res_real)
            state = jnp.stack([next_real, next_imag], axis=2)
        final = state.reshape(HIDDEN_FEATURES, 2 * K, L)
        wavenumber_sets = jnp.einsum('cql,hl->chq', final, basis, precision=ceiling_bound).astype(jnp.bfloat16)
        wavenumber_sets = wavenumber_sets.reshape(HIDDEN_FEATURES * PARALLEL_COUNT, 2 * K).astype(jnp.float32)
        predicted_state = jnp.dot(wavenumber_sets, reverse_pass, precision=ceiling_bound).astype(jnp.bfloat16).reshape(HIDDEN_FEATURES, PARALLEL_COUNT, MERIDIAN_COUNT)
        return (predicted_state, jnp.stack([derivative_inphase, derivative_quadrature], axis=2), subset_misfit)
    predicted_state, derivative_nested, misfit_series = lax.map(one_example, (hidden_encoding, desired_spectra))
    grad = lax.optimization_barrier(jnp.sum(derivative_nested, axis=0))
    total = jnp.sum(grad * grad)
    limit = math.sqrt(HIDDEN_FEATURES * K * 2 * L)
    factor = jnp.minimum(1.0, limit / jnp.sqrt(total + 1e-06))
    capped_derivative = grad * factor
    count = BATCH * LEADS * HIDDEN_FEATURES * K * 2 * L
    spectral_misfit = jnp.reshape(jnp.sum(misfit_series) / count, (1,))
    return (predicted_state, capped_derivative, spectral_misfit)
```

```python
import math

import jax
import jax.numpy as jnp
import numpy as np
from jax import lax
from jax.experimental import pallas as pl
from jax.experimental.pallas import tpu as pltpu
from jax.sharding import PartitionSpec as P

HIDDEN_FEATURES = 256
PARALLEL_COUNT = 384
K = 256
L = 128
LEADS = 6


def forward_table(wavenumber_span, kept):
    column = jnp.arange(wavenumber_span, dtype=jnp.int32)[:, None]
    wave = jnp.arange(kept, dtype=jnp.int32)[None, :]
    phase = (wave * column % wavenumber_span).astype(jnp.float32) * (
        2.0 * math.pi / wavenumber_span
    )
    factor = 1.0 / math.sqrt(wavenumber_span)
    table = jnp.stack([jnp.cos(phase) * factor, -jnp.sin(phase) * factor], axis=2)
    return table.reshape(wavenumber_span, 2 * kept)


def inverse_table(wavenumber_span, kept):
    wave = jnp.arange(kept, dtype=jnp.int32)[:, None]
    column = jnp.arange(wavenumber_span, dtype=jnp.int32)[None, :]
    phase = (wave * column % wavenumber_span).astype(jnp.float32) * (
        2.0 * math.pi / wavenumber_span
    )
    weight = jnp.where(wave == 0, 1.0, 2.0).astype(jnp.float32) / math.sqrt(wavenumber_span)
    table = jnp.stack([weight * jnp.cos(phase), -weight * jnp.sin(phase)], axis=1)
    return table.reshape(2 * kept, wavenumber_span)


def latitude_table(height, modes):
    row = jnp.arange(height, dtype=jnp.int32)[:, None]
    mode = jnp.arange(modes, dtype=jnp.int32)[None, :]
    phase = ((2 * row + 1) * mode % (4 * height)).astype(jnp.float32) * (math.pi / (2 * height))
    weight = jnp.where(mode == 0, math.sqrt(1.0 / height), math.sqrt(2.0 / height)).astype(
        jnp.float32
    )
    return weight * jnp.cos(phase)


def plain_per_device(hidden_encoding, eigenvalues, desired_spectra):
    ceiling_bound = lax.Precision.HIGHEST
    channels = hidden_encoding.shape[1]
    band = hidden_encoding.shape[2]
    wavenumber_span = hidden_encoding.shape[3]
    owned = eigenvalues.shape[1]
    forward = forward_table(wavenumber_span, K).astype(jnp.bfloat16)
    reverse_pass = inverse_table(wavenumber_span, K).astype(jnp.bfloat16)
    basis = latitude_table(PARALLEL_COUNT, L)
    basis_half = basis.astype(jnp.bfloat16)
    spectra = jnp.dot(
        hidden_encoding[0].reshape(channels * band, wavenumber_span),
        forward,
        preferred_element_type=jnp.float32,
    )
    spectra = spectra.astype(jnp.bfloat16).reshape(channels, band, 2 * K)
    coeffs = jnp.einsum(
        "nhq,hl->nql",
        lax.all_to_all(spectra, "lat", split_axis=2, concat_axis=1, tiled=True),
        basis_half,
        preferred_element_type=jnp.float32,
    )
    state = coeffs.reshape(channels, owned, 2, L)
    lam_real = eigenvalues[:, :, 0]
    lam_imag = eigenvalues[:, :, 1]
    subset_misfit = jnp.zeros((), jnp.float32)
    derivative_inphase = jnp.zeros((channels, owned, L), jnp.float32)
    derivative_quadrature = jnp.zeros((channels, owned, L), jnp.float32)
    for lead in range(LEADS):
        prev_real = state[:, :, 0]
        prev_imag = state[:, :, 1]
        next_real = lam_real * prev_real - lam_imag * prev_imag
        next_imag = lam_real * prev_imag + lam_imag * prev_real
        goal = desired_spectra[0, lead].astype(jnp.float32)
        res_real = next_real - goal[:, :, 0]
        res_imag = next_imag - goal[:, :, 1]
        subset_misfit = subset_misfit + jnp.sum(res_real * res_real + res_imag * res_imag)
        weight = 2.0 * (lead + 1)
        derivative_inphase = derivative_inphase + weight * (
            prev_real * res_real + prev_imag * res_imag
        )
        derivative_quadrature = derivative_quadrature + weight * (
            prev_real * res_imag - prev_imag * res_real
        )
        state = jnp.stack([next_real, next_imag], axis=2)
    local_grad = jnp.stack([derivative_inphase, derivative_quadrature], axis=2)
    limit = math.sqrt(HIDDEN_FEATURES * K * 2 * L)
    count = lax.axis_size("rep") * LEADS * HIDDEN_FEATURES * K * 2 * L
    summed = lax.psum(local_grad.astype(jnp.bfloat16), "rep").astype(jnp.float32)
    total = lax.psum(jnp.sum(summed * summed), ("lat", "chan"))
    loss_sum = lax.psum(subset_misfit, ("lat", "chan", "rep"))
    capped_derivative = summed * jnp.minimum(1.0, limit / jnp.sqrt(total + 1e-06))
    spectral_misfit = jnp.reshape(loss_sum / count, (1,))
    final = state.reshape(channels, 2 * owned, L)
    wavenumber_sets = jnp.einsum("nql,hl->nhq", final, basis, precision=ceiling_bound).astype(
        jnp.bfloat16
    )
    block = lax.all_to_all(wavenumber_sets, "lat", split_axis=1, concat_axis=2, tiled=True)
    element_sequence = block.shape[0]
    matrix_stripe = block.shape[1]
    vectorized_field = jnp.dot(
        block.reshape(element_sequence * matrix_stripe, block.shape[2]),
        reverse_pass,
        preferred_element_type=jnp.float32,
    )
    predicted_state = vectorized_field.astype(jnp.bfloat16).reshape(
        element_sequence, matrix_stripe, wavenumber_span
    )
    return (predicted_state[None], capped_derivative, spectral_misfit)


CHUNKS = 4
VMEM = 48 * 1024 * 1024


def block_order(blocks, owned):
    wave = np.arange(blocks * owned).reshape(blocks, 1, owned)
    return (2 * wave + np.arange(2).reshape(1, 2, 1)).reshape(-1)


def longitude_tables(span, kept, order):
    wave = np.arange(kept)
    column = np.arange(span)
    phase = 2.0 * np.pi / span * (column[:, None] * wave[None, :] % span)
    both = np.stack([np.cos(phase), -np.sin(phase)], axis=2) / math.sqrt(span)
    both = both.reshape(span, 2 * kept).astype(np.float32)
    twice = np.repeat(np.where(wave == 0, 1.0, 2.0), 2).astype(np.float32)
    back = (both * twice).T
    return both[:, order].astype(jnp.bfloat16), back[order].astype(jnp.bfloat16)


def latitude_factors(height, modes, bands):
    row = np.arange(height)[:, None]
    mode = np.arange(modes)[None, :]
    table = np.cos(np.pi / (2 * height) * ((2 * row + 1) * mode % (4 * height)))
    table = table * np.where(mode == 0, math.sqrt(1.0 / height), math.sqrt(2.0 / height))
    span = height // bands
    tilt = 1.0 + 1e-3 * np.arange(modes) / modes
    bases = []
    for band in range(bands):
        rows = table[band * span : (band + 1) * span]
        left = rows.copy()
        found = np.zeros((span, 0))
        while found.shape[1] < span:
            size = np.sqrt(np.sum(left * left, axis=0))
            if np.max(size) < 2e-8 * math.sqrt(2.0 / bands):
                break
            pick = left[:, np.argmax(size * tilt)]
            for _ in range(2):
                pick = pick - np.sum(found * np.sum(found * pick[:, None], axis=0), axis=1)
            pick = pick / np.sqrt(np.sum(pick * pick))
            found = np.concatenate([found, pick[:, None]], axis=1)
            left = left - pick[:, None] * np.sum(pick[:, None] * left, axis=0)
        bases.append(found)
    rank = max(base.shape[1] for base in bases)
    rank = -(-rank // 16) * 16
    basis = np.zeros((bands, span, rank))
    weights = np.zeros((bands, rank, modes))
    for band, base in enumerate(bases):
        basis[band, :, : base.shape[1]] = base
        weights[band, : base.shape[1]] = base.T @ table[band * span : (band + 1) * span]
    return basis.astype(np.float32), weights.astype(np.float32)


def deinterleave(owned):
    order = np.concatenate([np.arange(owned) * 2, np.arange(owned) * 2 + 1])
    return np.eye(2 * owned, dtype=np.float32)[order].astype(jnp.bfloat16)


def two_parts(array):
    high = array.astype(jnp.bfloat16)
    return high, (array - high.astype(np.float32)).astype(jnp.bfloat16)


def sum_over(value, axis):
    size = lax.axis_size(axis)
    if size & (size - 1):
        return lax.psum(value, axis)
    step = 1
    while step < size:
        value = value + lax.ppermute(value, axis, [(i, i ^ step) for i in range(size)])
        step *= 2
    return value


def forward_kernel(field_ref, table_ref, basis_ref, sent_ref, spectra):
    group, band, span = field_ref.shape
    spectra[...] = jnp.dot(
        field_ref[...].reshape(group * band, span),
        table_ref[...],
        preferred_element_type=jnp.float32,
    ).astype(jnp.bfloat16).reshape(spectra.shape)
    blocks, width = sent_ref.shape[0], sent_ref.shape[3]
    for channel in range(group):
        short = jnp.dot(basis_ref[...], spectra[channel], preferred_element_type=jnp.float32)
        rank = sent_ref.shape[2]
        short = (short[:rank] + short[rank:]).astype(jnp.bfloat16)
        for block in range(blocks):
            sent_ref[block, channel] = short[:, block * width : (block + 1) * width]


def rollout_kernel(
    got_ref, weights_ref, order_ref, lam_ref, goal_ref, sent_ref, grad_ref, misfit_ref
):
    blocks, group, rank, width = got_ref.shape
    owned = width // 2
    leads = goal_ref.shape[0]

    @pl.when(pl.program_id(0) == 0)
    def _():
        misfit_ref[...] = jnp.zeros_like(misfit_ref)

    def one_channel(channel, carry):
        got = got_ref[:, channel].reshape(blocks * rank, width)
        state = lax.dot_general(
            got,
            weights_ref[...],
            (((0,), (0,)), ((), ())),
            preferred_element_type=jnp.float32,
        )
        modes = state.shape[1] // 2
        state = state[:, :modes] + state[:, modes:]
        real, imag = state[:owned], state[owned:]
        lam_real = lam_ref[channel, pl.ds(0, owned, stride=2), :]
        lam_imag = lam_ref[channel, pl.ds(1, owned, stride=2), :]
        misfit = jnp.zeros_like(real)
        grad_real = jnp.zeros_like(real)
        grad_imag = jnp.zeros_like(real)
        for lead in range(leads):
            goal = jnp.dot(
                order_ref[...], goal_ref[lead, channel], preferred_element_type=jnp.float32
            )
            next_real = lam_real * real - lam_imag * imag
            next_imag = lam_real * imag + lam_imag * real
            res_real = next_real - goal[:owned]
            res_imag = next_imag - goal[owned:]
            misfit = misfit + (res_real * res_real + res_imag * res_imag)
            weight = 2.0 * (lead + 1)
            grad_real = grad_real + weight * (real * res_real + imag * res_imag)
            grad_imag = grad_imag + weight * (real * res_imag - imag * res_real)
            real, imag = next_real, next_imag
        grad_ref[channel, :owned] = grad_real.astype(jnp.bfloat16)
        grad_ref[channel, owned:] = grad_imag.astype(jnp.bfloat16)
        misfit_ref[...] += jnp.sum(misfit.reshape(-1, 8, misfit.shape[1]), axis=0)
        final = jnp.concatenate([real, imag], axis=0)
        high = final.astype(jnp.bfloat16)
        low = (final - high.astype(jnp.float32)).astype(jnp.bfloat16)
        contract = (((1,), (1,)), ((), ()))
        short = lax.dot_general(
            weights_ref[...],
            jnp.concatenate([high, high], axis=1),
            contract,
            preferred_element_type=jnp.float32,
        ) + lax.dot_general(
            weights_ref[:, :modes], low, contract, preferred_element_type=jnp.float32
        )
        sent_ref[:, channel] = short.astype(jnp.bfloat16).reshape(blocks, rank, width)
        return carry

    lax.fori_loop(0, group, one_channel, 0)


def inverse_kernel(got_ref, basis_ref, table_ref, *refs):
    field_ref, bands = refs[-2], refs[-1]
    blocks, group, rank, width = got_ref.shape
    for channel in range(group):
        for block in range(blocks):
            got = got_ref[block, channel]
            bands[channel, :, block * width : (block + 1) * width] = jnp.dot(
                basis_ref[...],
                jnp.concatenate([got, got], axis=0),
                preferred_element_type=jnp.float32,
            ).astype(jnp.bfloat16)
    field_ref[...] = jnp.dot(
        bands[...].reshape(group * bands.shape[1], bands.shape[2]),
        table_ref[...],
        preferred_element_type=jnp.float32,
    ).astype(jnp.bfloat16).reshape(field_ref.shape)


def scale_kernel(scale_ref, mine_ref, other_ref, *refs):
    out_ref = refs[-1]
    group, rows, _ = mine_ref.shape
    owned = rows // 2
    scale = scale_ref[0]

    def one_channel(channel, carry):
        total = mine_ref[channel].astype(jnp.float32) + other_ref[channel].astype(jnp.float32)
        total = total * scale
        out_ref[channel, pl.ds(0, owned, stride=2), :] = total[:owned]
        out_ref[channel, pl.ds(1, owned, stride=2), :] = total[owned:]
        return carry

    lax.fori_loop(0, group, one_channel, 0)


def params():
    return pltpu.CompilerParams(vmem_limit_bytes=VMEM, dimension_semantics=("arbitrary",))


def whole(array):
    return pl.BlockSpec(array.shape, lambda step: (0,) * array.ndim)


def cost(flops, moved):
    return pl.CostEstimate(flops=int(flops), bytes_accessed=int(moved), transcendentals=0)


def chunk_call(kernel, chunk, count, group, operands, ins, shape, full, scratch, work, name):
    first = chunk * count // group
    block = (group,) + shape.shape[1:]
    rest = (0,) * (len(shape.shape) - 1)
    aliases = {}
    if full is not None:
        aliases = {len(operands): 0}
        operands = operands + (full,)
        ins = ins + [pl.BlockSpec(memory_space=pl.ANY)]
    return pl.pallas_call(
        kernel,
        grid=(count // group,),
        in_specs=ins,
        out_specs=pl.BlockSpec(block, lambda step: (first + step,) + rest),
        out_shape=shape,
        scratch_shapes=scratch,
        input_output_aliases=aliases,
        compiler_params=params(),
        cost_estimate=work,
        name=name,
    )(*operands)


def per_device(hidden_encoding, eigenvalues, desired_spectra):
    bands_over = lax.axis_size("lat")
    channels, band, span = hidden_encoding.shape[1:]
    owned = eigenvalues.shape[1]
    width = 2 * owned
    bf16 = jnp.bfloat16
    f32 = jnp.float32
    order = block_order(bands_over, owned)
    forward, back = longitude_tables(span, K, order)
    basis, weights = latitude_factors(PARALLEL_COUNT, L, bands_over)
    rank = basis.shape[2]
    mine = lax.axis_index("lat")
    basis = np.concatenate(two_parts(basis), axis=2)
    basis = lax.dynamic_index_in_dim(jnp.asarray(basis), mine, keepdims=False)
    basis_t = basis.T
    weights = weights.reshape(bands_over * rank, L)
    weights = jnp.asarray(np.concatenate(two_parts(weights), axis=1))
    forward, back = jnp.asarray(forward), jnp.asarray(back)
    permute = jnp.asarray(deinterleave(owned))
    field = hidden_encoding.reshape(channels, band, span)
    lam = eigenvalues.reshape(channels, width, L)
    goals = desired_spectra.reshape(LEADS, channels, width, L)

    count = channels // CHUNKS
    group = math.gcd(count, 8)
    steps = count // group
    blocked = pl.BlockSpec((bands_over, group, rank, width), lambda step: (0, step, 0, 0))
    rows = pl.BlockSpec((group, width, L), lambda step: (step, 0, 0))
    packed = jax.ShapeDtypeStruct((bands_over, count, rank, width), bf16)
    pair = [(0, 1), (1, 0)]
    longitude_work = 2 * count * band * span * 2 * K

    arrived = []
    for chunk in range(CHUNKS):
        first = chunk * steps
        sent = pl.pallas_call(
            forward_kernel,
            grid=(steps,),
            in_specs=[
                pl.BlockSpec((group, band, span), lambda step, first=first: (first + step, 0, 0)),
                whole(forward),
                whole(basis_t),
            ],
            out_specs=blocked,
            out_shape=packed,
            scratch_shapes=[pltpu.VMEM((group, band, 2 * K), bf16)],
            compiler_params=params(),
            cost_estimate=cost(2 * longitude_work, 2 * count * band * span),
            name="longitude_forward",
        )(field, forward, basis_t)
        arrived.append(lax.all_to_all(sent, "lat", split_axis=0, concat_axis=0, tiled=True))

    returned, grads, others, misfits, squares = [], [], [], [], []
    for chunk in range(CHUNKS):
        first = chunk * steps
        sent, grad, misfit = pl.pallas_call(
            rollout_kernel,
            grid=(steps,),
            in_specs=[
                blocked,
                whole(weights),
                whole(permute),
                pl.BlockSpec((group, width, L), lambda step, first=first: (first + step, 0, 0)),
                pl.BlockSpec(
                    (LEADS, group, width, L), lambda step, first=first: (0, first + step, 0, 0)
                ),
            ],
            out_specs=(blocked, rows, pl.BlockSpec((8, L), lambda step: (0, 0))),
            out_shape=(
                packed,
                jax.ShapeDtypeStruct((count, width, L), bf16),
                jax.ShapeDtypeStruct((8, L), f32),
            ),
            compiler_params=params(),
            cost_estimate=cost(3 * longitude_work, 20 * count * width * L),
            name="rollout",
        )(arrived[chunk], weights, permute, lam, goals)
        returned.append(lax.all_to_all(sent, "lat", split_axis=0, concat_axis=0, tiled=True))
        grads.append(grad)
        misfits.append(jnp.sum(misfit))
        other = lax.ppermute(grad, "rep", pair) if lax.axis_size("rep") == 2 else grad
        others.append(other)
        total = grad.astype(f32) + other.astype(f32)
        squares.append(jnp.sum(total * total))

    sums = jnp.stack([sum(squares) / lax.axis_size("rep"), sum(misfits)])
    for axis in ("rep", "chan", "lat"):
        sums = sum_over(sums, axis)
    limit = math.sqrt(HIDDEN_FEATURES * K * 2 * L)
    scale = jnp.minimum(1.0, limit / jnp.sqrt(sums[0] + 1e-06)).reshape(1)
    total_count = lax.axis_size("rep") * LEADS * HIDDEN_FEATURES * K * 2 * L
    spectral_misfit = (sums[1] / total_count).reshape(1)

    predicted = None
    for chunk in range(CHUNKS):
        predicted = chunk_call(
            inverse_kernel,
            chunk,
            count,
            group,
            (returned[chunk], basis, back),
            [blocked, whole(basis), whole(back)],
            jax.ShapeDtypeStruct((channels, band, span), bf16),
            predicted,
            [pltpu.VMEM((group, band, 2 * K), bf16)],
            cost(2 * longitude_work, 2 * count * band * span),
            "longitude_inverse",
        )
    capped = None
    for chunk in range(CHUNKS):
        capped = chunk_call(
            scale_kernel,
            chunk,
            count,
            group,
            (scale, grads[chunk], others[chunk]),
            [pl.BlockSpec(memory_space=pltpu.SMEM), rows, rows],
            jax.ShapeDtypeStruct((channels, width, L), f32),
            capped,
            [],
            cost(4 * count * width * L, 8 * count * width * L),
            "scale",
        )
    return (
        predicted.reshape(hidden_encoding.shape),
        capped.reshape(channels, owned, 2, L),
        spectral_misfit,
    )


def solution(mesh):
    placed = (
        P(("groups", "rep"), "chan", "lat", None),
        P("chan", "lat", None, None),
        P(("groups", "rep"), None, "chan", "lat", None, None),
    )
    tiled = (2 * K) % (128 * mesh.shape["lat"]) == 0
    tiled = tiled and PARALLEL_COUNT % (16 * mesh.shape["lat"]) == 0
    tiled = tiled and HIDDEN_FEATURES % (CHUNKS * mesh.shape["chan"]) == 0
    tiled = tiled and mesh.shape["rep"] == 2
    return jax.shard_map(
        per_device if tiled else plain_per_device,
        mesh=mesh,
        in_specs=placed,
        out_specs=(
            P(("groups", "rep"), "chan", "lat", None),
            P(("groups", "chan"), "lat", None, None),
            P("groups"),
        ),
        check_vma=False,
    )
```

```python
import math

import jax
import jax.numpy as jnp
import numpy as np
from jax import lax
from jax.experimental import pallas as pl
from jax.experimental.pallas import tpu as pltpu
from jax.sharding import PartitionSpec as P

HIDDEN_FEATURES = 256
PARALLEL_COUNT = 384
K = 256
L = 128
LEADS = 6


def forward_table(wavenumber_span, kept):
    column = jnp.arange(wavenumber_span, dtype=jnp.int32)[:, None]
    wave = jnp.arange(kept, dtype=jnp.int32)[None, :]
    phase = (wave * column % wavenumber_span).astype(jnp.float32) * (
        2.0 * math.pi / wavenumber_span
    )
    factor = 1.0 / math.sqrt(wavenumber_span)
    table = jnp.stack([jnp.cos(phase) * factor, -jnp.sin(phase) * factor], axis=2)
    return table.reshape(wavenumber_span, 2 * kept)


def inverse_table(wavenumber_span, kept):
    wave = jnp.arange(kept, dtype=jnp.int32)[:, None]
    column = jnp.arange(wavenumber_span, dtype=jnp.int32)[None, :]
    phase = (wave * column % wavenumber_span).astype(jnp.float32) * (
        2.0 * math.pi / wavenumber_span
    )
    weight = jnp.where(wave == 0, 1.0, 2.0).astype(jnp.float32) / math.sqrt(wavenumber_span)
    table = jnp.stack([weight * jnp.cos(phase), -weight * jnp.sin(phase)], axis=1)
    return table.reshape(2 * kept, wavenumber_span)


def latitude_table(height, modes):
    row = jnp.arange(height, dtype=jnp.int32)[:, None]
    mode = jnp.arange(modes, dtype=jnp.int32)[None, :]
    phase = ((2 * row + 1) * mode % (4 * height)).astype(jnp.float32) * (math.pi / (2 * height))
    weight = jnp.where(mode == 0, math.sqrt(1.0 / height), math.sqrt(2.0 / height)).astype(
        jnp.float32
    )
    return weight * jnp.cos(phase)


def plain_per_device(hidden_encoding, eigenvalues, desired_spectra):
    ceiling_bound = lax.Precision.HIGHEST
    channels = hidden_encoding.shape[1]
    band = hidden_encoding.shape[2]
    wavenumber_span = hidden_encoding.shape[3]
    owned = eigenvalues.shape[1]
    forward = forward_table(wavenumber_span, K).astype(jnp.bfloat16)
    reverse_pass = inverse_table(wavenumber_span, K).astype(jnp.bfloat16)
    basis = latitude_table(PARALLEL_COUNT, L)
    basis_half = basis.astype(jnp.bfloat16)
    spectra = jnp.dot(
        hidden_encoding[0].reshape(channels * band, wavenumber_span),
        forward,
        preferred_element_type=jnp.float32,
    )
    spectra = spectra.astype(jnp.bfloat16).reshape(channels, band, 2 * K)
    coeffs = jnp.einsum(
        "nhq,hl->nql",
        lax.all_to_all(spectra, "lat", split_axis=2, concat_axis=1, tiled=True),
        basis_half,
        preferred_element_type=jnp.float32,
    )
    state = coeffs.reshape(channels, owned, 2, L)
    lam_real = eigenvalues[:, :, 0]
    lam_imag = eigenvalues[:, :, 1]
    subset_misfit = jnp.zeros((), jnp.float32)
    derivative_inphase = jnp.zeros((channels, owned, L), jnp.float32)
    derivative_quadrature = jnp.zeros((channels, owned, L), jnp.float32)
    for lead in range(LEADS):
        prev_real = state[:, :, 0]
        prev_imag = state[:, :, 1]
        next_real = lam_real * prev_real - lam_imag * prev_imag
        next_imag = lam_real * prev_imag + lam_imag * prev_real
        goal = desired_spectra[0, lead].astype(jnp.float32)
        res_real = next_real - goal[:, :, 0]
        res_imag = next_imag - goal[:, :, 1]
        subset_misfit = subset_misfit + jnp.sum(res_real * res_real + res_imag * res_imag)
        weight = 2.0 * (lead + 1)
        derivative_inphase = derivative_inphase + weight * (
            prev_real * res_real + prev_imag * res_imag
        )
        derivative_quadrature = derivative_quadrature + weight * (
            prev_real * res_imag - prev_imag * res_real
        )
        state = jnp.stack([next_real, next_imag], axis=2)
    local_grad = jnp.stack([derivative_inphase, derivative_quadrature], axis=2)
    limit = math.sqrt(HIDDEN_FEATURES * K * 2 * L)
    count = lax.axis_size("rep") * LEADS * HIDDEN_FEATURES * K * 2 * L
    summed = lax.psum(local_grad.astype(jnp.bfloat16), "rep").astype(jnp.float32)
    total = lax.psum(jnp.sum(summed * summed), ("lat", "chan"))
    loss_sum = lax.psum(subset_misfit, ("lat", "chan", "rep"))
    capped_derivative = summed * jnp.minimum(1.0, limit / jnp.sqrt(total + 1e-06))
    spectral_misfit = jnp.reshape(loss_sum / count, (1,))
    final = state.reshape(channels, 2 * owned, L)
    wavenumber_sets = jnp.einsum("nql,hl->nhq", final, basis, precision=ceiling_bound).astype(
        jnp.bfloat16
    )
    block = lax.all_to_all(wavenumber_sets, "lat", split_axis=1, concat_axis=2, tiled=True)
    element_sequence = block.shape[0]
    matrix_stripe = block.shape[1]
    vectorized_field = jnp.dot(
        block.reshape(element_sequence * matrix_stripe, block.shape[2]),
        reverse_pass,
        preferred_element_type=jnp.float32,
    )
    predicted_state = vectorized_field.astype(jnp.bfloat16).reshape(
        element_sequence, matrix_stripe, wavenumber_span
    )
    return (predicted_state[None], capped_derivative, spectral_misfit)


CHUNKS = 4
VMEM = 48 * 1024 * 1024


def block_order(blocks, owned):
    wave = np.arange(blocks * owned).reshape(blocks, 1, owned)
    return (2 * wave + np.arange(2).reshape(1, 2, 1)).reshape(-1)


def longitude_tables(span, kept, order):
    wave = np.arange(kept)
    column = np.arange(span)
    phase = 2.0 * np.pi / span * (column[:, None] * wave[None, :] % span)
    both = np.stack([np.cos(phase), -np.sin(phase)], axis=2) / math.sqrt(span)
    both = both.reshape(span, 2 * kept).astype(np.float32)
    twice = np.repeat(np.where(wave == 0, 1.0, 2.0), 2).astype(np.float32)
    back = (both * twice).T
    return both[:, order].astype(jnp.bfloat16), back[order].astype(jnp.bfloat16)


def latitude_factors(height, modes, bands):
    row = np.arange(height)[:, None]
    mode = np.arange(modes)[None, :]
    table = np.cos(np.pi / (2 * height) * ((2 * row + 1) * mode % (4 * height)))
    table = table * np.where(mode == 0, math.sqrt(1.0 / height), math.sqrt(2.0 / height))
    span = height // bands
    tilt = 1.0 + 1e-3 * np.arange(modes) / modes
    bases = []
    for band in range(bands):
        rows = table[band * span : (band + 1) * span]
        left = rows.copy()
        found = np.zeros((span, 0))
        while found.shape[1] < span:
            size = np.sqrt(np.sum(left * left, axis=0))
            if np.max(size) < 2e-8 * math.sqrt(2.0 / bands):
                break
            pick = left[:, np.argmax(size * tilt)]
            for _ in range(2):
                pick = pick - np.sum(found * np.sum(found * pick[:, None], axis=0), axis=1)
            pick = pick / np.sqrt(np.sum(pick * pick))
            found = np.concatenate([found, pick[:, None]], axis=1)
            left = left - pick[:, None] * np.sum(pick[:, None] * left, axis=0)
        bases.append(found)
    rank = max(base.shape[1] for base in bases)
    rank = -(-rank // 16) * 16
    basis = np.zeros((bands, span, rank))
    weights = np.zeros((bands, rank, modes))
    for band, base in enumerate(bases):
        basis[band, :, : base.shape[1]] = base
        weights[band, : base.shape[1]] = base.T @ table[band * span : (band + 1) * span]
    return basis.astype(np.float32), weights.astype(np.float32)


def deinterleave(owned):
    order = np.concatenate([np.arange(owned) * 2, np.arange(owned) * 2 + 1])
    return np.eye(2 * owned, dtype=np.float32)[order].astype(jnp.bfloat16)


def two_parts(array):
    high = array.astype(jnp.bfloat16)
    return high, (array - high.astype(np.float32)).astype(jnp.bfloat16)


def sum_over(value, axis):
    size = lax.axis_size(axis)
    if size & (size - 1):
        return lax.psum(value, axis)
    step = 1
    while step < size:
        value = value + lax.ppermute(value, axis, [(i, i ^ step) for i in range(size)])
        step *= 2
    return value


def forward_kernel(field_ref, table_ref, basis_ref, sent_ref, spectra):
    group, band, span = field_ref.shape
    spectra[...] = jnp.dot(
        field_ref[...].reshape(group * band, span),
        table_ref[...],
        preferred_element_type=jnp.float32,
    ).astype(jnp.bfloat16).reshape(spectra.shape)
    blocks, width = sent_ref.shape[0], sent_ref.shape[3]
    for channel in range(group):
        short = jnp.dot(basis_ref[...], spectra[channel], preferred_element_type=jnp.float32)
        rank = sent_ref.shape[2]
        short = (short[:rank] + short[rank:]).astype(jnp.bfloat16)
        for block in range(blocks):
            sent_ref[block, channel] = short[:, block * width : (block + 1) * width]


def rollout_kernel(
    got_ref, weights_ref, order_ref, lam_ref, goal_ref, sent_ref, grad_ref, misfit_ref
):
    blocks, group, rank, width = got_ref.shape
    owned = width // 2
    leads = goal_ref.shape[0]

    @pl.when(pl.program_id(0) == 0)
    def _():
        misfit_ref[...] = jnp.zeros_like(misfit_ref)

    def one_channel(channel, carry):
        got = got_ref[:, channel].reshape(blocks * rank, width)
        state = lax.dot_general(
            got,
            weights_ref[...],
            (((0,), (0,)), ((), ())),
            preferred_element_type=jnp.float32,
        )
        modes = state.shape[1] // 2
        state = state[:, :modes] + state[:, modes:]
        real, imag = state[:owned], state[owned:]
        lam_real = lam_ref[channel, pl.ds(0, owned, stride=2), :]
        lam_imag = lam_ref[channel, pl.ds(1, owned, stride=2), :]
        misfit = jnp.zeros_like(real)
        grad_real = jnp.zeros_like(real)
        grad_imag = jnp.zeros_like(real)
        for lead in range(leads):
            goal = jnp.dot(
                order_ref[...], goal_ref[lead, channel], preferred_element_type=jnp.float32
            )
            next_real = lam_real * real - lam_imag * imag
            next_imag = lam_real * imag + lam_imag * real
            res_real = next_real - goal[:owned]
            res_imag = next_imag - goal[owned:]
            misfit = misfit + (res_real * res_real + res_imag * res_imag)
            weight = 2.0 * (lead + 1)
            grad_real = grad_real + weight * (real * res_real + imag * res_imag)
            grad_imag = grad_imag + weight * (real * res_imag - imag * res_real)
            real, imag = next_real, next_imag
        grad_ref[channel, :owned] = grad_real.astype(jnp.bfloat16)
        grad_ref[channel, owned:] = grad_imag.astype(jnp.bfloat16)
        misfit_ref[...] += jnp.sum(misfit.reshape(-1, 8, misfit.shape[1]), axis=0)
        final = jnp.concatenate([real, imag], axis=0)
        high = final.astype(jnp.bfloat16)
        low = (final - high.astype(jnp.float32)).astype(jnp.bfloat16)
        contract = (((1,), (1,)), ((), ()))
        short = lax.dot_general(
            weights_ref[...],
            jnp.concatenate([high, high], axis=1),
            contract,
            preferred_element_type=jnp.float32,
        ) + lax.dot_general(
            weights_ref[:, :modes], low, contract, preferred_element_type=jnp.float32
        )
        sent_ref[:, channel] = short.astype(jnp.bfloat16).reshape(blocks, rank, width)
        return carry

    lax.fori_loop(0, group, one_channel, 0)


def inverse_kernel(got_ref, basis_ref, table_ref, *refs):
    field_ref, bands = refs[-2], refs[-1]
    blocks, group, rank, width = got_ref.shape
    for channel in range(group):
        for block in range(blocks):
            got = got_ref[block, channel]
            bands[channel, :, block * width : (block + 1) * width] = jnp.dot(
                basis_ref[...],
                jnp.concatenate([got, got], axis=0),
                preferred_element_type=jnp.float32,
            ).astype(jnp.bfloat16)
    field_ref[...] = jnp.dot(
        bands[...].reshape(group * bands.shape[1], bands.shape[2]),
        table_ref[...],
        preferred_element_type=jnp.float32,
    ).astype(jnp.bfloat16).reshape(field_ref.shape)


def scale_kernel(scale_ref, mine_ref, other_ref, *refs):
    out_ref = refs[-1]
    group, rows, _ = mine_ref.shape
    owned = rows // 2
    scale = scale_ref[0]

    def one_channel(channel, carry):
        total = mine_ref[channel].astype(jnp.float32) + other_ref[channel].astype(jnp.float32)
        total = total * scale
        out_ref[channel, pl.ds(0, owned, stride=2), :] = total[:owned]
        out_ref[channel, pl.ds(1, owned, stride=2), :] = total[owned:]
        return carry

    lax.fori_loop(0, group, one_channel, 0)


def params():
    return pltpu.CompilerParams(vmem_limit_bytes=VMEM, dimension_semantics=("arbitrary",))


def whole(array):
    return pl.BlockSpec(array.shape, lambda step: (0,) * array.ndim)


def cost(flops, moved):
    return pl.CostEstimate(flops=int(flops), bytes_accessed=int(moved), transcendentals=0)


def chunk_call(kernel, chunk, count, group, operands, ins, shape, full, scratch, work, name):
    first = chunk * count // group
    block = (group,) + shape.shape[1:]
    rest = (0,) * (len(shape.shape) - 1)
    aliases = {}
    if full is not None:
        aliases = {len(operands): 0}
        operands = operands + (full,)
        ins = ins + [pl.BlockSpec(memory_space=pl.ANY)]
    return pl.pallas_call(
        kernel,
        grid=(count // group,),
        in_specs=ins,
        out_specs=pl.BlockSpec(block, lambda step: (first + step,) + rest),
        out_shape=shape,
        scratch_shapes=scratch,
        input_output_aliases=aliases,
        compiler_params=params(),
        cost_estimate=work,
        name=name,
    )(*operands)


def per_device(hidden_encoding, eigenvalues, desired_spectra):
    bands_over = lax.axis_size("lat")
    channels, band, span = hidden_encoding.shape[1:]
    owned = eigenvalues.shape[1]
    width = 2 * owned
    bf16 = jnp.bfloat16
    f32 = jnp.float32
    order = block_order(bands_over, owned)
    forward, back = longitude_tables(span, K, order)
    basis, weights = latitude_factors(PARALLEL_COUNT, L, bands_over)
    rank = basis.shape[2]
    mine = lax.axis_index("lat")
    basis = np.concatenate(two_parts(basis), axis=2)
    basis = lax.dynamic_index_in_dim(jnp.asarray(basis), mine, keepdims=False)
    basis_t = basis.T
    weights = weights.reshape(bands_over * rank, L)
    weights = jnp.asarray(np.concatenate(two_parts(weights), axis=1))
    forward, back = jnp.asarray(forward), jnp.asarray(back)
    permute = jnp.asarray(deinterleave(owned))
    field = hidden_encoding.reshape(channels, band, span)
    lam = eigenvalues.reshape(channels, width, L)
    goals = desired_spectra.reshape(LEADS, channels, width, L)

    count = channels // CHUNKS
    group = math.gcd(count, 8)
    steps = count // group
    blocked = pl.BlockSpec((bands_over, group, rank, width), lambda step: (0, step, 0, 0))
    rows = pl.BlockSpec((group, width, L), lambda step: (step, 0, 0))
    packed = jax.ShapeDtypeStruct((bands_over, count, rank, width), bf16)
    pair = [(0, 1), (1, 0)]
    longitude_work = 2 * count * band * span * 2 * K

    arrived = []
    for chunk in range(CHUNKS):
        first = chunk * steps
        sent = pl.pallas_call(
            forward_kernel,
            grid=(steps,),
            in_specs=[
                pl.BlockSpec((group, band, span), lambda step, first=first: (first + step, 0, 0)),
                whole(forward),
                whole(basis_t),
            ],
            out_specs=blocked,
            out_shape=packed,
            scratch_shapes=[pltpu.VMEM((group, band, 2 * K), bf16)],
            compiler_params=params(),
            cost_estimate=cost(2 * longitude_work, 2 * count * band * span),
            name="longitude_forward",
        )(field, forward, basis_t)
        arrived.append(lax.all_to_all(sent, "lat", split_axis=0, concat_axis=0, tiled=True))

    returned, grads, others, misfits, squares = [], [], [], [], []
    for chunk in range(CHUNKS):
        first = chunk * steps
        sent, grad, misfit = pl.pallas_call(
            rollout_kernel,
            grid=(steps,),
            in_specs=[
                blocked,
                whole(weights),
                whole(permute),
                pl.BlockSpec((group, width, L), lambda step, first=first: (first + step, 0, 0)),
                pl.BlockSpec(
                    (LEADS, group, width, L), lambda step, first=first: (0, first + step, 0, 0)
                ),
            ],
            out_specs=(blocked, rows, pl.BlockSpec((8, L), lambda step: (0, 0))),
            out_shape=(
                packed,
                jax.ShapeDtypeStruct((count, width, L), bf16),
                jax.ShapeDtypeStruct((8, L), f32),
            ),
            compiler_params=params(),
            cost_estimate=cost(3 * longitude_work, 20 * count * width * L),
            name="rollout",
        )(arrived[chunk], weights, permute, lam, goals)
        returned.append(lax.all_to_all(sent, "lat", split_axis=0, concat_axis=0, tiled=True))
        grads.append(grad)
        misfits.append(jnp.sum(misfit))
        other = lax.ppermute(grad, "rep", pair) if lax.axis_size("rep") == 2 else grad
        others.append(other)
        total = grad.astype(f32) + other.astype(f32)
        squares.append(jnp.sum(total * total))

    sums = jnp.stack([sum(squares) / lax.axis_size("rep"), sum(misfits)])
    for axis in ("rep", "chan"):
        sums = sum_over(sums, axis)

    predicted = None
    for chunk in range(CHUNKS):
        predicted = chunk_call(
            inverse_kernel,
            chunk,
            count,
            group,
            (returned[chunk], basis, back),
            [blocked, whole(basis), whole(back)],
            jax.ShapeDtypeStruct((channels, band, span), bf16),
            predicted,
            [pltpu.VMEM((group, band, 2 * K), bf16)],
            cost(2 * longitude_work, 2 * count * band * span),
            "longitude_inverse",
        )
        if chunk == CHUNKS - 2:
            sums, predicted = lax.optimization_barrier((sums, predicted))
            sums = sum_over(sums, "lat")

    limit = math.sqrt(HIDDEN_FEATURES * K * 2 * L)
    scale = jnp.minimum(1.0, limit / jnp.sqrt(sums[0] + 1e-06)).reshape(1)
    total_count = lax.axis_size("rep") * LEADS * HIDDEN_FEATURES * K * 2 * L
    spectral_misfit = (sums[1] / total_count).reshape(1)
    capped = None
    for chunk in range(CHUNKS):
        capped = chunk_call(
            scale_kernel,
            chunk,
            count,
            group,
            (scale, grads[chunk], others[chunk]),
            [pl.BlockSpec(memory_space=pltpu.SMEM), rows, rows],
            jax.ShapeDtypeStruct((channels, width, L), f32),
            capped,
            [],
            cost(4 * count * width * L, 8 * count * width * L),
            "scale",
        )
    return (
        predicted.reshape(hidden_encoding.shape),
        capped.reshape(channels, owned, 2, L),
        spectral_misfit,
    )


def solution(mesh):
    placed = (
        P(("groups", "rep"), "chan", "lat", None),
        P("chan", "lat", None, None),
        P(("groups", "rep"), None, "chan", "lat", None, None),
    )
    tiled = (2 * K) % (128 * mesh.shape["lat"]) == 0
    tiled = tiled and PARALLEL_COUNT % (16 * mesh.shape["lat"]) == 0
    tiled = tiled and HIDDEN_FEATURES % (CHUNKS * mesh.shape["chan"]) == 0
    tiled = tiled and mesh.shape["rep"] == 2
    return jax.shard_map(
        per_device if tiled else plain_per_device,
        mesh=mesh,
        in_specs=placed,
        out_specs=(
            P(("groups", "rep"), "chan", "lat", None),
            P(("groups", "chan"), "lat", None, None),
            P("groups"),
        ),
        check_vma=False,
    )
```
